32 devices in a mesh: occ: 4 (over y, x), vir: 8 (over z, core).
Axes of the slice: x: 2, y: 2, z: 4, core: 2. Of those that a mesh axis runs over, the one named last changes fastest.
Arguments:
- amplitudes: bfloat16 [4096, 16384], P('occ', 'vir'), may hold values from -6 to 6
- integrals: bfloat16 [16384, 2048], P('vir', 'occ'), may hold values from -0.1875 to 0.1875
- ij_irrep: int32 [4096], P('occ'), may hold values from 0 to 7
- cd_irrep: int32 [16384], P('vir'), may hold values from 0 to 7
Outputs:
- ladder: float32 [4096, 2048], P('occ', 'vir')
The draws below stay inside these ranges and needn't reach their ends.
All inputs are finite; a program needn't handle non-finite values.
Results may differ from the reference program's by a relative error of at most 0.0003.
Values may be sent and summed in bfloat16 or wider, within the bound.
No kernel may reach another device: no remote copies, remote signals or barrier semaphores. Data moves between devices by JAX's collectives and lax.ppermute only.
A program may use at most 64 MiB of HBM per device.

```python
import jax
import jax.numpy as jnp
from jax import lax

NAB = 2048
NIJ = 4096
NCD = 16384


def with_ends(array, rng, least, top_value):
    shape = array.shape
    spot = [jax.random.randint(jax.random.fold_in(rng, axis), (), 0, shape[axis]) for axis in range(len(shape))]
    array = array.at[tuple(spot)].set(least)
    longest = shape.index(max(shape))
    spot[longest] = (spot[longest] + 1) % shape[longest]
    return array.at[tuple(spot)].set(top_value)


def raised(drawn, rng, source, target, blocks, factor):
    def block_of(axis_at):
        return (jnp.arange(drawn.shape[axis_at]) // (drawn.shape[axis_at] // blocks)).reshape((-1,) + (1,) * (drawn.ndim - 1 - axis_at))

    first = jax.random.permutation(rng, blocks)[block_of(target)]
    other_side = (block_of(target) + blocks // 2) % blocks
    return jnp.where((block_of(source) == first) | (block_of(source) == other_side), factor * drawn, drawn)


def block_scale(own_key, dims, shards, low, top_value):
    def one(dim, parts):
        heights = jax.random.uniform(jax.random.fold_in(jax.random.fold_in(own_key, 6), dim), (parts,), jnp.float32, low / len(shards), top_value / len(shards))
        return jnp.repeat(jnp.exp(heights), dims[dim] // parts).reshape((-1,) + (1,) * (len(dims) - dim - 1))

    level = one(*shards[0])
    for cut in shards[1:]:
        level = level * one(*cut)
    return level


def gaussian(stream_key, extent, scale, most, split=(), held_as=jnp.bfloat16):
    entries = jax.random.normal(stream_key, extent, jnp.float32) * scale
    if len(split) > 0:
        entries = block_scale(stream_key, extent, split, -0.22, 0.18) * entries
    return jnp.clip(entries, min=-most, max=most).astype(held_as)


def heavy_noise(rng, extent, width, most, shards, heavy, kind=jnp.bfloat16):
    values = width * jax.random.normal(rng, extent, jnp.float32)
    if shards:
        values = values * block_scale(rng, extent, shards, -0.22, 0.18)
    return jnp.clip(raised(values, jax.random.fold_in(rng, 3), *heavy), -most, most).astype(kind)


def setup_inputs(seed: int = 0) -> dict:
    seeds = jax.random.split(jax.random.key(seed), 5)
    amplitudes = gaussian(seeds[0], (NIJ, NCD), 1.0, 6.0, ((0, 4), (1, 8)))
    integrals = heavy_noise(seeds[1], (NCD, NAB), (NCD // 8) ** -0.5, 0.1875, ((0, 8), (1, 4)), (0, 1, 8, 2.0))
    ij_irrep = with_ends(jax.random.randint(seeds[2], (NIJ,), 0, 8), jax.random.fold_in(seeds[2], 1), 0, 7).astype(jnp.int32)
    cd_irrep = with_ends(jax.random.randint(seeds[3], (NCD,), 0, 8), jax.random.fold_in(seeds[3], 1), 0, 7).astype(jnp.int32)
    return {"amplitudes": amplitudes, "integrals": integrals, "ij_irrep": ij_irrep, "cd_irrep": cd_irrep}


def reference(amplitudes, integrals, ij_irrep, cd_irrep):
    block_rows = min(1024, amplitudes.shape[0])
    blocks = amplitudes.shape[0] // block_rows
    amp_blocks = amplitudes.reshape(blocks, block_rows, amplitudes.shape[1])
    irrep_blocks = ij_irrep.reshape(blocks, block_rows)

    def one_block(pair):
        rows, labels = pair
        masked = jnp.where(labels[:, None] == cd_irrep[None, :], rows, jnp.zeros_like(rows))
        return jnp.dot(masked, integrals, preferred_element_type=jnp.float32)

    result = lax.map(one_block, (amp_blocks, irrep_blocks))
    return result.reshape(amplitudes.shape[0], integrals.shape[1])
```

```python
import functools
import math

import jax
import jax.numpy as jnp
from jax import lax
from jax.experimental import pallas as pl
from jax.experimental.pallas import tpu as pltpu
from jax.sharding import PartitionSpec as P

AMPLITUDE_MAX = 6.0
INTEGRAL_MAX = 0.1875
HALF_MAX = 65504.0
GRANULES = 4
ROW_TILE = 256
VMEM_LIMIT = 32 * 1024 * 1024


def masked_amplitudes(amplitudes, ij_irrep, cd_irrep):
    return jnp.where(
        ij_irrep[:, None] == cd_irrep[None, :], amplitudes, jnp.zeros_like(amplitudes)
    )


def plain_body(amplitudes, integrals, ij_irrep, cd_irrep):
    partial_sums = jnp.dot(
        masked_amplitudes(amplitudes, ij_irrep, cd_irrep),
        lax.all_gather(integrals, "occ", axis=1, tiled=True),
        preferred_element_type=jnp.float32,
    )
    return lax.psum_scatter(partial_sums, "vir", scatter_dimension=1, tiled=True)


def product_kernel(scale, occ_ref, own_amps, other_amps, *refs):
    pieces, out_ref, own_rows, other_rows = refs[:8], refs[8], refs[9], refs[10]
    half = own_rows.shape[0] // 2
    width = pieces[0].shape[1] // 2

    @pl.when(pl.program_id(0) == 0)
    def _():
        for part in range(2):
            rows = pl.ds(part * half, half)
            blocks = [piece[...] for piece in pieces[part::2]]
            own_rows[rows, :] = jnp.concatenate([b[:, :width] for b in blocks], axis=1)
            other_rows[rows, :] = jnp.concatenate([b[:, width:] for b in blocks], axis=1)

    sums = jnp.dot(own_amps[...], own_rows[...], preferred_element_type=jnp.float32)
    sums += jnp.dot(other_amps[...], other_rows[...], preferred_element_type=jnp.float32)
    sums = sums * scale
    top = sums.shape[0] // 2
    for relation in range(4):
        block = sums[:, relation * width : (relation + 1) * width]
        packed = jnp.concatenate([block[:top], block[top:]], axis=1)
        out_ref[occ_ref[0] ^ relation] = packed


def product(occ, own_amps, other_amps, halves, scale):
    rows, depth = own_amps.shape
    lanes = halves[0][0].shape[1]
    in_specs = [
        pl.BlockSpec(memory_space=pltpu.SMEM),
        pl.BlockSpec((ROW_TILE, depth), lambda i: (i, 0)),
        pl.BlockSpec((ROW_TILE, depth), lambda i: (i, 0)),
    ]
    for _, part in halves:
        in_specs.append(pl.BlockSpec((depth // 2, lanes), functools.partial(lambda at, i: (at, 0), part)))
    return pl.pallas_call(
        functools.partial(product_kernel, scale),
        grid=(rows // ROW_TILE,),
        in_specs=in_specs,
        out_specs=pl.BlockSpec((4, ROW_TILE // 2, lanes), lambda i: (0, i, 0)),
        out_shape=jax.ShapeDtypeStruct((4, rows // 2, lanes), jnp.float32),
        scratch_shapes=[pltpu.VMEM((depth, 2 * lanes), jnp.bfloat16)] * 2,
        compiler_params=pltpu.CompilerParams(vmem_limit_bytes=VMEM_LIMIT),
        cost_estimate=pl.CostEstimate(
            flops=4 * rows * depth * 2 * lanes, bytes_accessed=4 * rows * depth, transcendentals=0
        ),
    )(occ, own_amps, other_amps, *[array for array, _ in halves])


def total_kernel(unscale, *refs):
    parts, out_ref = refs[:-1], refs[-1]
    columns = []
    for part in parts:
        total = part[...] * unscale
        width = total.shape[1] // 2
        columns.append(jnp.concatenate([total[:, :width], total[:, width:]], axis=0))
    out_ref[...] = jnp.concatenate(columns, axis=1)


def total(parts, unscale):
    rows, lanes = parts[0].shape
    return pl.pallas_call(
        functools.partial(total_kernel, unscale),
        grid=(2 * rows // ROW_TILE,),
        in_specs=[pl.BlockSpec((ROW_TILE // 2, lanes), lambda i: (i, 0))] * len(parts),
        out_specs=pl.BlockSpec((ROW_TILE, lanes // 2 * len(parts)), lambda i: (i, 0)),
        out_shape=jax.ShapeDtypeStruct((2 * rows, lanes // 2 * len(parts)), jnp.float32),
        compiler_params=pltpu.CompilerParams(vmem_limit_bytes=VMEM_LIMIT),
    )(*parts)


def solution(mesh):
    occ_size, vir_size = mesh.shape["occ"], mesh.shape["vir"]
    chips_z = vir_size // 2

    def send(array, target):
        pairs = [
            (o * vir_size + v, target(o, v)[0] * vir_size + target(o, v)[1])
            for o in range(occ_size)
            for v in range(vir_size)
        ]
        return lax.ppermute(array, ("occ", "vir"), pairs)

    to_x = functools.partial(send, target=lambda o, v: (o ^ 1, v))
    to_y = functools.partial(send, target=lambda o, v: (o ^ 2, v))
    to_core = functools.partial(send, target=lambda o, v: (o, v ^ 1))

    def body(amplitudes, integrals, ij_irrep, cd_irrep):
        depth, columns = integrals.shape
        width = columns // 2
        step = width // GRANULES
        bound = 2 * depth * AMPLITUDE_MAX * INTEGRAL_MAX
        scale = 2.0 ** math.floor(math.log2(HALF_MAX / bound))
        occ = lax.axis_index("occ").astype(jnp.int32).reshape(1)
        core = lax.axis_index("vir") % 2

        mine = lax.dynamic_slice_in_dim(integrals, core * width, width, axis=1)
        theirs = lax.dynamic_slice_in_dim(integrals, (1 - core) * width, width, axis=1)
        swapped = to_core(theirs)
        own_amps = masked_amplitudes(amplitudes, ij_irrep, cd_irrep)
        other_amps = to_core(own_amps)

        received = []
        for g in range(GRANULES):
            cut = slice(g * step, (g + 1) * step)
            own = jnp.concatenate([mine[:, cut], swapped[:, cut]], axis=1)
            top, bottom = own[: depth // 2], own[depth // 2 :]
            if g < GRANULES - 1:
                from_x, from_y = to_x(own), to_y(own)
                x_halves = [(from_x, 0), (from_x, 1)]
                y_halves = [(from_y, 0), (from_y, 1)]
                x_top, y_bottom = from_x[: depth // 2], from_y[depth // 2 :]
            else:
                x_top, y_bottom = to_x(top), to_y(bottom)
                x_halves = [(x_top, 0), (to_x(bottom), 0)]
                y_halves = [(to_y(top), 0), (y_bottom, 0)]
            far = [(to_y(x_top), 0), (to_x(y_bottom), 0)]
            halves = [(own, 0), (own, 1)] + x_halves + y_halves + far
            partials = product(occ, own_amps, other_amps, halves, scale)
            groups = [[z * 2 + k for z in range(chips_z)] for k in range(2)]
            arrived = lax.all_to_all(
                partials.astype(jnp.float16), "vir", 0, 0, axis_index_groups=groups, tiled=True
            )
            received.append(arrived.astype(jnp.float32).sum(axis=0))
        return total(received, 1.0 / scale)

    special = occ_size == 4 and vir_size == 8
    in_specs = (P("occ", "vir"), P("vir", "occ"), P("occ"), P("vir"))
    return jax.shard_map(
        body if special else plain_body,
        mesh=mesh,
        in_specs=in_specs,
        out_specs=P("occ", "vir"),
        check_vma=False,
    )
```

```python
import functools
import math

import jax
import jax.numpy as jnp
from jax import lax
from jax.experimental import pallas as pl
from jax.experimental.pallas import tpu as pltpu
from jax.sharding import PartitionSpec as P

AMPLITUDE_MAX = 6.0
INTEGRAL_MAX = 0.1875
HALF_MAX = 65504.0
SHARES = (1, 1, 1, 1)
ORDER = (('near', 0), ('rest', 0), ('near', 1), ('far', 0), ('rest', 1), ('near', 2), ('far', 1), ('rest', 2), ('near', 3), ('far', 2), ('rest', 3), ('far', 3))
DEPTH = 4
STRICT = 1
ZMODE = ('pair', 'pair', 'pair', 'pair')
RAW_SWAP = True
SWAP_CUTS = 1
SWAP_WHOLE = True
LATE = False
GATES = {('far', 1): [('product', 0)], ('far', 2): [('product', 1)], ('rest', 3): [('pair', 0)], ('product', 2): [('pair', 1)], ('product', 3): [('product', 2)], ('near', 2): ['masked']}
ROW_TILE = 256
VMEM_LIMIT = 14680064


def masked_amplitudes(amplitudes, ij_irrep, cd_irrep):
    rows, columns = ij_irrep.astype(amplitudes.dtype), cd_irrep.astype(amplitudes.dtype)
    return jnp.where(rows[:, None] == columns[None, :], amplitudes, jnp.zeros_like(amplitudes))


def in_vmem(array):
    return pltpu.with_memory_space_constraint(array, pltpu.VMEM)


def plain_body(amplitudes, integrals, ij_irrep, cd_irrep):
    partial_sums = jnp.dot(
        masked_amplitudes(amplitudes, ij_irrep, cd_irrep),
        lax.all_gather(integrals, "occ", axis=1, tiled=True),
        preferred_element_type=jnp.float32,
    )
    return lax.psum_scatter(partial_sums, "vir", scatter_dimension=1, tiled=True)


def product_kernel(scale, slot_ref, own_amps, other_amps, *refs):
    pieces, out_ref, own_rows, other_rows = refs[:8], refs[8], refs[9], refs[10]
    depth, width = own_rows.shape[0], own_rows.shape[1] // 4
    folds = depth // pieces[0].shape[0]
    part = depth // folds
    for target, blocks in ((own_rows, pieces[0::2]), (other_rows, pieces[1::2])):
        for f in range(folds):
            cut = slice(f * width, (f + 1) * width)
            target[pl.ds(f * part, part), :] = jnp.concatenate([b[:, cut] for b in blocks], axis=1)

    for i in range(own_amps.shape[0] // ROW_TILE):
        at = pl.ds(i * ROW_TILE, ROW_TILE)
        sums = jnp.dot(own_amps[at, :], own_rows[...], preferred_element_type=jnp.float32)
        sums += jnp.dot(other_amps[at, :], other_rows[...], preferred_element_type=jnp.float32)
        sums = sums * scale
        rows = ROW_TILE // folds
        for relation in range(4):
            block = sums[:, relation * width : (relation + 1) * width]
            if folds > 1:
                block = jnp.concatenate([block[f * rows : (f + 1) * rows] for f in range(folds)], axis=1)
            out_ref[slot_ref[relation], pl.ds(i * rows, rows), :] = block


def product(slots, own_amps, other_amps, pieces, scale, depth):
    lanes = pieces[0].shape[1]
    folds = depth // pieces[0].shape[0]
    return pl.pallas_call(
        functools.partial(product_kernel, scale),
        in_specs=[pl.BlockSpec(memory_space=pltpu.SMEM)]
        + [pl.BlockSpec(memory_space=pltpu.VMEM)] * (2 + len(pieces)),
        out_specs=pl.BlockSpec(memory_space=pltpu.VMEM),
        out_shape=jax.ShapeDtypeStruct((4, own_amps.shape[0] // folds, lanes), jnp.float32),
        scratch_shapes=[pltpu.VMEM((depth, 4 * lanes // folds), jnp.bfloat16)] * 2,
        compiler_params=pltpu.CompilerParams(vmem_limit_bytes=VMEM_LIMIT),
        cost_estimate=pl.CostEstimate(flops=0, bytes_accessed=0, transcendentals=0),
    )(slots, own_amps, other_amps, *pieces)


def total_kernel(unscale, *refs):
    parts, out_ref = refs[:-1], refs[-1]
    rows = out_ref.shape[0]
    for i in range(rows // ROW_TILE):
        columns = []
        for part in parts:
            folds = rows // part.shape[0]
            tile = ROW_TILE // folds
            total = part[pl.ds(i * tile, tile), :] * unscale
            width = total.shape[1] // folds
            if folds > 1:
                total = jnp.concatenate([total[:, f * width : (f + 1) * width] for f in range(folds)], axis=0)
            columns.append(total)
        out_ref[pl.ds(i * ROW_TILE, ROW_TILE), :] = jnp.concatenate(columns, axis=1)


def total(parts, unscale, rows, columns):
    return pl.pallas_call(
        functools.partial(total_kernel, unscale),
        in_specs=[pl.BlockSpec(memory_space=pltpu.VMEM)] * len(parts),
        out_specs=pl.BlockSpec(memory_space=pltpu.VMEM),
        out_shape=jax.ShapeDtypeStruct((rows, columns), jnp.float32),
        compiler_params=pltpu.CompilerParams(vmem_limit_bytes=VMEM_LIMIT),
        cost_estimate=pl.CostEstimate(flops=0, bytes_accessed=0, transcendentals=0),
    )(*parts)


def solution(mesh):
    occ_size, vir_size = mesh.shape["occ"], mesh.shape["vir"]
    chips_z = vir_size // 2

    def send(array, target):
        pairs = [
            (o * vir_size + v, target(o, v)[0] * vir_size + target(o, v)[1])
            for o in range(occ_size)
            for v in range(vir_size)
        ]
        return lax.ppermute(array, ("occ", "vir"), pairs)

    to_x = functools.partial(send, target=lambda o, v: (o ^ 1, v))
    to_y = functools.partial(send, target=lambda o, v: (o ^ 2, v))
    to_x_across = functools.partial(send, target=lambda o, v: (o ^ 1, v ^ 1))
    to_y_across = functools.partial(send, target=lambda o, v: (o ^ 2, v ^ 1))
    to_core = functools.partial(send, target=lambda o, v: (o, v ^ 1))

    def along_z(array, hop):
        return send(array, lambda o, v: (o, v ^ (2 * hop)))

    def body(amplitudes, integrals, ij_irrep, cd_irrep):
        depth, columns = integrals.shape
        width = columns // 2
        bound = 2 * depth * AMPLITUDE_MAX * INTEGRAL_MAX
        scale = 2.0 ** math.floor(math.log2(HALF_MAX / bound))
        core = lax.axis_index("vir") % 2
        chip = lax.axis_index("vir") // 2
        owners = lax.axis_index("occ") ^ jnp.arange(4, dtype=jnp.int32)
        hops = owners ^ chip
        ends = [width * sum(SHARES[: g + 1]) // sum(SHARES) for g in range(len(SHARES))]
        granules = range(len(SHARES))

        def piece(array, g):
            cut = array[:, (ends[g - 1] if g else 0) : ends[g]]
            if cut.shape[1] % 128 == 0:
                return cut
            folds = 128 // cut.shape[1]
            return jnp.concatenate(jnp.split(cut, folds), axis=1)

        def columns_of(array, which):
            return lax.dynamic_slice_in_dim(array, which * width, width, axis=1)

        first = (piece(columns_of(integrals, core), 0), piece(columns_of(integrals, 1 - core), 0))
        first, integrals = lax.optimization_barrier((first, integrals))
        mine, theirs = columns_of(integrals, core), columns_of(integrals, 1 - core)
        theirs_late, cd_late = theirs, cd_irrep
        if RAW_SWAP:
            cut = amplitudes.shape[0] // SWAP_CUTS
            chunks = [to_core(amplitudes[at : at + cut]) for at in range(0, amplitudes.shape[0], cut)]
            other_raw = jnp.concatenate(chunks, axis=0) if SWAP_CUTS > 1 else chunks[0]
            if LATE:
                theirs_late, cd_late, other_raw = lax.optimization_barrier((theirs, cd_irrep, other_raw))
            own_amps = masked_amplitudes(amplitudes, ij_irrep, cd_irrep)
            other_amps = masked_amplitudes(other_raw, ij_irrep, to_core(cd_late))
        else:
            if LATE:
                amplitudes, _ = lax.optimization_barrier((amplitudes, first))
            own_amps = masked_amplitudes(amplitudes, ij_irrep, cd_irrep)
            other_amps = to_core(own_amps)
        same = [first[0]] + [piece(mine, g) for g in granules[1:]]
        cross = [first[1]] + [piece(theirs, g) for g in granules[1:]]
        if SWAP_WHOLE:
            swapped = to_core(theirs_late)
            swapped = [piece(swapped, g) for g in granules]
        else:
            swapped = [to_core(block) for block in cross]

        values, on_x, on_y, sums = {"masked": (own_amps, other_amps)}, {}, {}, {}
        order = list(ORDER)

        def gated(load, name):
            waits = [values[other] for other in GATES.get(name, ()) if other in values]
            return lax.optimization_barrier((load, waits))[0] if waits else load

        for kind, g in ORDER:
            if kind == "far":
                loads = (on_y["near", g], on_x["near", g])
                ways = (to_x, to_y)
            elif kind == "near":
                loads = (same[g], cross[g])
                ways = (to_x, to_y_across)
            else:
                loads = (cross[g], same[g])
                ways = (to_x_across, to_y)
            loads = gated(loads, (kind, g))
            back = order.index((kind, g)) - DEPTH
            if back >= 0:
                earlier = [values[name] for name in order[max(back - STRICT, 0) : back + 1]]
                loads, _ = lax.optimization_barrier((loads, earlier))
            on_x[kind, g], on_y[kind, g] = ways[0](loads[0]), ways[1](loads[1])
            values[kind, g] = (on_x[kind, g], on_y[kind, g])
            if not all((k, g) in on_x for k in ("near", "rest", "far")):
                continue
            pieces = [
                same[g], swapped[g],
                on_x["near", g], on_x["rest", g],
                on_y["rest", g], on_y["near", g],
                on_y["far", g], on_x["far", g],
            ]
            pieces = gated(pieces, ("product", g))
            pairwise = ZMODE[g] == "pair"
            slots = hops // 2 + 2 * (hops % 2) if pairwise else owners if ZMODE[g] == "swap" else hops
            partials = product(slots, own_amps, other_amps, pieces, scale, depth)
            values["product", g] = partials
            if pairwise:
                kept, sent = partials[:2], partials[2:].astype(jnp.float16)
                pair = kept + along_z(sent, 1).astype(jnp.float32)
                values["pair", g] = pair
                sums[g] = pair[0] + along_z(pair[1].astype(jnp.float16), 2).astype(jnp.float32)
            elif ZMODE[g] == "swap":
                groups = [[z * 2 + k for z in range(chips_z)] for k in range(2)]
                halved = partials.astype(jnp.float16)
                arrived = lax.all_to_all(halved, "vir", 0, 0, axis_index_groups=groups, tiled=True)
                sums[g] = arrived.astype(jnp.float32).sum(axis=0)
            else:
                halved = partials.astype(jnp.float16)
                sums[g] = partials[0]
                for hop in range(1, chips_z):
                    arrived = along_z(halved[hop], hop)
                    if hop == 1:
                        values["pair", g] = arrived
                    sums[g] += arrived.astype(jnp.float32)
            values["sum", g] = sums[g]
        return total([sums[g] for g in granules], 1.0 / scale, amplitudes.shape[0], width)

    special = occ_size == 4 and vir_size == 8
    in_specs = (P("occ", "vir"), P("vir", "occ"), P("occ"), P("vir"))
    return jax.shard_map(
        body if special else plain_body,
        mesh=mesh,
        in_specs=in_specs,
        out_specs=P("occ", "vir"),
        check_vma=False,
    )
```

```python
import functools
import math

import jax
import jax.numpy as jnp
from jax import lax
from jax.experimental import pallas as pl
from jax.experimental.pallas import tpu as pltpu
from jax.sharding import PartitionSpec as P

AMPLITUDE_MAX = 6.0
INTEGRAL_MAX = 0.1875
HALF_MAX = 65504.0
SHARES = (2, 2, 2, 2)
ORDER = (('near', 0), ('rest', 0), ('near', 1), ('far', 0), ('rest', 1), ('near', 2), ('far', 1), ('rest', 2), ('near', 3), ('far', 2), ('rest', 3), ('far', 3))
DEPTH = 4
STRICT = 1
ZSPLIT = (1, 1, 2, 2)
GATES = {('far', 1): [('product', 0)], ('far', 2): [('product', 1)], ('rest', 3): [('pair', 0)], ('product', 2): [('pair', 1)], ('product', 3): [('product', 2)], ('near', 2): ['masked']}
ROW_TILE = 512
VMEM_LIMIT = 14 * 1024 * 1024


def masked_amplitudes(amplitudes, ij_irrep, cd_irrep):
    rows, columns = ij_irrep.astype(amplitudes.dtype), cd_irrep.astype(amplitudes.dtype)
    return jnp.where(rows[:, None] == columns[None, :], amplitudes, jnp.zeros_like(amplitudes))


def plain_body(amplitudes, integrals, ij_irrep, cd_irrep):
    partial_sums = jnp.dot(
        masked_amplitudes(amplitudes, ij_irrep, cd_irrep),
        lax.all_gather(integrals, "occ", axis=1, tiled=True),
        preferred_element_type=jnp.float32,
    )
    return lax.psum_scatter(partial_sums, "vir", scatter_dimension=1, tiled=True)


def product_kernel(scale, slot_ref, own_amps, other_amps, *refs):
    pieces, out_ref, own_rows, other_rows = refs[:8], refs[8], refs[9], refs[10]
    depth, width = own_rows.shape[0], own_rows.shape[1] // 4
    folds = depth // pieces[0].shape[0]
    part = depth // folds
    for target, blocks in ((own_rows, pieces[0::2]), (other_rows, pieces[1::2])):
        for f in range(folds):
            cut = slice(f * width, (f + 1) * width)
            target[pl.ds(f * part, part), :] = jnp.concatenate([b[:, cut] for b in blocks], axis=1)

    for i in range(own_amps.shape[0] // ROW_TILE):
        at = pl.ds(i * ROW_TILE, ROW_TILE)
        sums = jnp.dot(own_amps[at, :], own_rows[...], preferred_element_type=jnp.float32)
        sums += jnp.dot(other_amps[at, :], other_rows[...], preferred_element_type=jnp.float32)
        sums = sums * scale
        rows = ROW_TILE // folds
        for relation in range(4):
            block = sums[:, relation * width : (relation + 1) * width]
            if folds > 1:
                block = jnp.concatenate([block[f * rows : (f + 1) * rows] for f in range(folds)], axis=1)
            out_ref[slot_ref[relation], pl.ds(i * rows, rows), :] = block


def product(slots, own_amps, other_amps, pieces, scale, depth):
    lanes = pieces[0].shape[1]
    folds = depth // pieces[0].shape[0]
    return pl.pallas_call(
        functools.partial(product_kernel, scale),
        in_specs=[pl.BlockSpec(memory_space=pltpu.SMEM)]
        + [pl.BlockSpec(memory_space=pltpu.VMEM)] * (2 + len(pieces)),
        out_specs=pl.BlockSpec(memory_space=pltpu.VMEM),
        out_shape=jax.ShapeDtypeStruct((4, own_amps.shape[0] // folds, lanes), jnp.float32),
        scratch_shapes=[pltpu.VMEM((depth, 4 * lanes // folds), jnp.bfloat16)] * 2,
        compiler_params=pltpu.CompilerParams(vmem_limit_bytes=VMEM_LIMIT),
        cost_estimate=pl.CostEstimate(flops=0, bytes_accessed=0, transcendentals=0),
    )(slots, own_amps, other_amps, *pieces)


def total_kernel(unscale, *refs):
    parts, out_ref = refs[:-1], refs[-1]
    rows = out_ref.shape[0]
    for i in range(rows // ROW_TILE):
        columns = []
        for part in parts:
            folds = rows // part.shape[0]
            tile = ROW_TILE // folds
            total = part[pl.ds(i * tile, tile), :] * unscale
            width = total.shape[1] // folds
            if folds > 1:
                total = jnp.concatenate([total[:, f * width : (f + 1) * width] for f in range(folds)], axis=0)
            columns.append(total)
        out_ref[pl.ds(i * ROW_TILE, ROW_TILE), :] = jnp.concatenate(columns, axis=1)


def total(parts, unscale, rows, columns):
    return pl.pallas_call(
        functools.partial(total_kernel, unscale),
        in_specs=[pl.BlockSpec(memory_space=pltpu.VMEM)] * len(parts),
        out_specs=pl.BlockSpec(memory_space=pltpu.VMEM),
        out_shape=jax.ShapeDtypeStruct((rows, columns), jnp.float32),
        compiler_params=pltpu.CompilerParams(vmem_limit_bytes=VMEM_LIMIT),
        cost_estimate=pl.CostEstimate(flops=0, bytes_accessed=0, transcendentals=0),
    )(*parts)


def solution(mesh):
    occ_size, vir_size = mesh.shape["occ"], mesh.shape["vir"]
    chips_z = vir_size // 2

    def send(array, target):
        pairs = [
            (o * vir_size + v, target(o, v)[0] * vir_size + target(o, v)[1])
            for o in range(occ_size)
            for v in range(vir_size)
        ]
        return lax.ppermute(array, ("occ", "vir"), pairs)

    to_x = functools.partial(send, target=lambda o, v: (o ^ 1, v))
    to_y = functools.partial(send, target=lambda o, v: (o ^ 2, v))
    to_x_across = functools.partial(send, target=lambda o, v: (o ^ 1, v ^ 1))
    to_y_across = functools.partial(send, target=lambda o, v: (o ^ 2, v ^ 1))
    to_core = functools.partial(send, target=lambda o, v: (o, v ^ 1))

    def along_z(array, hop):
        return send(array, lambda o, v: (o, v ^ (2 * hop)))

    def body(amplitudes, integrals, ij_irrep, cd_irrep):
        depth, columns = integrals.shape
        width = columns // 2
        bound = 4 * depth * AMPLITUDE_MAX * INTEGRAL_MAX
        scale = 2.0 ** math.floor(math.log2(HALF_MAX / bound))
        core = lax.axis_index("vir") % 2
        chip = lax.axis_index("vir") // 2
        owners = lax.axis_index("occ") ^ jnp.arange(4, dtype=jnp.int32)
        hops = owners ^ chip
        ends = [width * sum(SHARES[: g + 1]) // sum(SHARES) for g in range(len(SHARES))]
        granules = range(len(SHARES))

        def piece(array, g):
            cut = array[:, (ends[g - 1] if g else 0) : ends[g]]
            if cut.shape[1] % 128 == 0:
                return cut
            folds = 128 // cut.shape[1]
            return jnp.concatenate(jnp.split(cut, folds), axis=1)

        def columns_of(array, which):
            return lax.dynamic_slice_in_dim(array, which * width, width, axis=1)

        first = (piece(columns_of(integrals, core), 0), piece(columns_of(integrals, 1 - core), 0))
        first, integrals = lax.optimization_barrier((first, integrals))
        mine, theirs = columns_of(integrals, core), columns_of(integrals, 1 - core)
        other_raw = to_core(amplitudes)
        own_amps = masked_amplitudes(amplitudes, ij_irrep, cd_irrep)
        other_amps = masked_amplitudes(other_raw, ij_irrep, to_core(cd_irrep))
        same = [first[0]] + [piece(mine, g) for g in granules[1:]]
        cross = [first[1]] + [piece(theirs, g) for g in granules[1:]]
        swapped = to_core(theirs)
        swapped = [piece(swapped, g) for g in granules]

        values, on_x, on_y, sums = {"masked": (own_amps, other_amps)}, {}, {}, {}
        order = list(ORDER)

        def gated(load, name):
            waits = [values[other] for other in GATES.get(name, ()) if other in values]
            return lax.optimization_barrier((load, waits))[0] if waits else load

        for kind, g in ORDER:
            if kind == "far":
                loads = (on_y["near", g], on_x["near", g])
                ways = (to_x, to_y)
            elif kind == "near":
                loads = (same[g], cross[g])
                ways = (to_x, to_y_across)
            else:
                loads = (cross[g], same[g])
                ways = (to_x_across, to_y)
            loads = gated(loads, (kind, g))
            back = order.index((kind, g)) - DEPTH
            if back >= 0:
                earlier = [values[name] for name in order[max(back - STRICT, 0) : back + 1]]
                loads, _ = lax.optimization_barrier((loads, earlier))
            on_x[kind, g], on_y[kind, g] = ways[0](loads[0]), ways[1](loads[1])
            values[kind, g] = (on_x[kind, g], on_y[kind, g])
            if not all((k, g) in on_x for k in ("near", "rest", "far")):
                continue
            pieces = [
                same[g], swapped[g],
                on_x["near", g], on_x["rest", g],
                on_y["rest", g], on_y["near", g],
                on_y["far", g], on_x["far", g],
            ]
            pieces = gated(pieces, ("product", g))
            slots = hops // 2 + 2 * (hops % 2)
            partials = product(slots, own_amps, other_amps, pieces, scale, depth)
            values["product", g] = partials
            parts = []
            for kept in jnp.split(partials, ZSPLIT[g], axis=1):
                pair = kept[:2] + along_z(kept[2:].astype(jnp.float16), 1).astype(jnp.float32)
                parts.append(pair[0] + along_z(pair[1].astype(jnp.float16), 2).astype(jnp.float32))
            values["pair", g] = pair
            sums[g] = jnp.concatenate(parts, axis=0) if len(parts) > 1 else parts[0]
            values["sum", g] = sums[g]
        return total([sums[g] for g in granules], 1.0 / scale, amplitudes.shape[0], width)

    special = occ_size == 4 and vir_size == 8
    in_specs = (P("occ", "vir"), P("vir", "occ"), P("occ"), P("vir"))
    return jax.shard_map(
        body if special else plain_body,
        mesh=mesh,
        in_specs=in_specs,
        out_specs=P("occ", "vir"),
        check_vma=False,
    )
```

```python
import functools
import math

import jax
import jax.numpy as jnp
from jax import lax
from jax.experimental import pallas as pl
from jax.experimental.pallas import tpu as pltpu
from jax.sharding import PartitionSpec as P

AMPLITUDE_MAX = 6.0
INTEGRAL_MAX = 0.1875
HALF_MAX = 65504.0
SHARES = (2, 2, 2, 2)
ORDER = (('near', 0), ('rest', 0), ('near', 1), ('far', 0), ('rest', 1), ('near', 2), ('far', 1), ('rest', 2), ('near', 3), ('far', 2), ('rest', 3), ('far', 3))
DEPTH = 4
STRICT = 1
ZSPLIT = (1, 1, 2, 2)
GATES = {('far', 1): [('product', 0)], ('far', 2): [('product', 1)], ('rest', 3): [('pair', 0)], ('product', 2): [('pair', 1)], ('product', 3): [('product', 2)], ('near', 2): ['masked']}
ROW_TILE = 1024
VMEM_LIMIT = 11 * 1024 * 1024


def masked_amplitudes(amplitudes, ij_irrep, cd_irrep):
    rows, columns = ij_irrep.astype(amplitudes.dtype), cd_irrep.astype(amplitudes.dtype)
    return jnp.where(rows[:, None] == columns[None, :], amplitudes, jnp.zeros_like(amplitudes))


def plain_body(amplitudes, integrals, ij_irrep, cd_irrep):
    partial_sums = jnp.dot(
        masked_amplitudes(amplitudes, ij_irrep, cd_irrep),
        lax.all_gather(integrals, "occ", axis=1, tiled=True),
        preferred_element_type=jnp.float32,
    )
    return lax.psum_scatter(partial_sums, "vir", scatter_dimension=1, tiled=True)


def product_kernel(scale, slot_ref, own_amps, other_amps, *refs):
    pieces, out_ref, own_rows, other_rows = refs[:8], refs[8], refs[9], refs[10]
    depth, width = own_rows.shape[0], own_rows.shape[1] // 4
    folds = depth // pieces[0].shape[0]
    part = depth // folds
    for target, blocks in ((own_rows, pieces[0::2]), (other_rows, pieces[1::2])):
        for f in range(folds):
            cut = slice(f * width, (f + 1) * width)
            target[pl.ds(f * part, part), :] = jnp.concatenate([b[:, cut] for b in blocks], axis=1)

    for i in range(own_amps.shape[0] // ROW_TILE):
        at = pl.ds(i * ROW_TILE, ROW_TILE)
        sums = jnp.dot(own_amps[at, :], own_rows[...], preferred_element_type=jnp.float32)
        sums += jnp.dot(other_amps[at, :], other_rows[...], preferred_element_type=jnp.float32)
        sums = sums * scale
        rows = ROW_TILE // folds
        for relation in range(4):
            block = sums[:, relation * width : (relation + 1) * width]
            if folds > 1:
                block = jnp.concatenate([block[f * rows : (f + 1) * rows] for f in range(folds)], axis=1)
            out_ref[slot_ref[relation], pl.ds(i * rows, rows), :] = block


def product(slots, own_amps, other_amps, pieces, scale, depth):
    lanes = pieces[0].shape[1]
    folds = depth // pieces[0].shape[0]
    return pl.pallas_call(
        functools.partial(product_kernel, scale),
        in_specs=[pl.BlockSpec(memory_space=pltpu.SMEM)]
        + [pl.BlockSpec(memory_space=pltpu.VMEM)] * (2 + len(pieces)),
        out_specs=pl.BlockSpec(memory_space=pltpu.VMEM),
        out_shape=jax.ShapeDtypeStruct((4, own_amps.shape[0] // folds, lanes), jnp.float32),
        scratch_shapes=[pltpu.VMEM((depth, 4 * lanes // folds), jnp.bfloat16)] * 2,
        compiler_params=pltpu.CompilerParams(vmem_limit_bytes=VMEM_LIMIT),
        cost_estimate=pl.CostEstimate(flops=0, bytes_accessed=0, transcendentals=0),
    )(slots, own_amps, other_amps, *pieces)


def total_kernel(unscale, *refs):
    parts, out_ref = refs[:-1], refs[-1]
    rows = out_ref.shape[0]
    for i in range(rows // ROW_TILE):
        columns = []
        for part in parts:
            folds = rows // part.shape[0]
            tile = ROW_TILE // folds
            total = part[pl.ds(i * tile, tile), :] * unscale
            width = total.shape[1] // folds
            if folds > 1:
                total = jnp.concatenate([total[:, f * width : (f + 1) * width] for f in range(folds)], axis=0)
            columns.append(total)
        out_ref[pl.ds(i * ROW_TILE, ROW_TILE), :] = jnp.concatenate(columns, axis=1)


def total(parts, unscale, rows, columns):
    return pl.pallas_call(
        functools.partial(total_kernel, unscale),
        in_specs=[pl.BlockSpec(memory_space=pltpu.VMEM)] * len(parts),
        out_specs=pl.BlockSpec(memory_space=pltpu.VMEM),
        out_shape=jax.ShapeDtypeStruct((rows, columns), jnp.float32),
        compiler_params=pltpu.CompilerParams(vmem_limit_bytes=VMEM_LIMIT),
        cost_estimate=pl.CostEstimate(flops=0, bytes_accessed=0, transcendentals=0),
    )(*parts)


def solution(mesh):
    occ_size, vir_size = mesh.shape["occ"], mesh.shape["vir"]
    chips_z = vir_size // 2

    def send(array, target):
        pairs = [
            (o * vir_size + v, target(o, v)[0] * vir_size + target(o, v)[1])
            for o in range(occ_size)
            for v in range(vir_size)
        ]
        return lax.ppermute(array, ("occ", "vir"), pairs)

    to_x = functools.partial(send, target=lambda o, v: (o ^ 1, v))
    to_y = functools.partial(send, target=lambda o, v: (o ^ 2, v))
    to_x_across = functools.partial(send, target=lambda o, v: (o ^ 1, v ^ 1))
    to_y_across = functools.partial(send, target=lambda o, v: (o ^ 2, v ^ 1))
    to_core = functools.partial(send, target=lambda o, v: (o, v ^ 1))

    def along_z(array, hop):
        return send(array, lambda o, v: (o, v ^ (2 * hop)))

    def body(amplitudes, integrals, ij_irrep, cd_irrep):
        depth, columns = integrals.shape
        width = columns // 2
        bound = 4 * depth * AMPLITUDE_MAX * INTEGRAL_MAX
        scale = 2.0 ** math.floor(math.log2(HALF_MAX / bound))
        core = lax.axis_index("vir") % 2
        chip = lax.axis_index("vir") // 2
        owners = lax.axis_index("occ") ^ jnp.arange(4, dtype=jnp.int32)
        hops = owners ^ chip
        ends = [width * sum(SHARES[: g + 1]) // sum(SHARES) for g in range(len(SHARES))]
        granules = range(len(SHARES))

        def piece(array, g):
            cut = array[:, (ends[g - 1] if g else 0) : ends[g]]
            if cut.shape[1] % 128 == 0:
                return cut
            folds = 128 // cut.shape[1]
            return jnp.concatenate(jnp.split(cut, folds), axis=1)

        def columns_of(array, which):
            return lax.dynamic_slice_in_dim(array, which * width, width, axis=1)

        first = (piece(columns_of(integrals, core), 0), piece(columns_of(integrals, 1 - core), 0))
        first, integrals = lax.optimization_barrier((first, integrals))
        mine, theirs = columns_of(integrals, core), columns_of(integrals, 1 - core)
        other_raw = to_core(amplitudes)
        own_amps = masked_amplitudes(amplitudes, ij_irrep, cd_irrep)
        other_amps = masked_amplitudes(other_raw, ij_irrep, to_core(cd_irrep))
        same = [first[0]] + [piece(mine, g) for g in granules[1:]]
        cross = [first[1]] + [piece(theirs, g) for g in granules[1:]]
        swapped = to_core(theirs)
        swapped = [piece(swapped, g) for g in granules]

        values, on_x, on_y, sums = {"masked": (own_amps, other_amps)}, {}, {}, {}
        order = list(ORDER)

        def gated(load, name):
            waits = [values[other] for other in GATES.get(name, ()) if other in values]
            return lax.optimization_barrier((load, waits))[0] if waits else load

        for kind, g in ORDER:
            if kind == "far":
                loads = (on_y["near", g], on_x["near", g])
                ways = (to_x, to_y)
            elif kind == "near":
                loads = (same[g], cross[g])
                ways = (to_x, to_y_across)
            else:
                loads = (cross[g], same[g])
                ways = (to_x_across, to_y)
            loads = gated(loads, (kind, g))
            back = order.index((kind, g)) - DEPTH
            if back >= 0:
                earlier = [values[name] for name in order[max(back - STRICT, 0) : back + 1]]
                loads, _ = lax.optimization_barrier((loads, earlier))
            on_x[kind, g], on_y[kind, g] = ways[0](loads[0]), ways[1](loads[1])
            values[kind, g] = (on_x[kind, g], on_y[kind, g])
            if not all((k, g) in on_x for k in ("near", "rest", "far")):
                continue
            pieces = [
                same[g], swapped[g],
                on_x["near", g], on_x["rest", g],
                on_y["rest", g], on_y["near", g],
                on_y["far", g], on_x["far", g],
            ]
            pieces = gated(pieces, ("product", g))
            slots = hops // 2 + 2 * (hops % 2)
            partials = product(slots, own_amps, other_amps, pieces, scale, depth)
            values["product", g] = partials
            parts = []
            for kept in jnp.split(partials, ZSPLIT[g], axis=1):
                pair = kept[:2] + along_z(kept[2:].astype(jnp.float16), 1).astype(jnp.float32)
                parts.append(pair[0] + along_z(pair[1].astype(jnp.float16), 2).astype(jnp.float32))
            values["pair", g] = pair
            sums[g] = jnp.concatenate(parts, axis=0) if len(parts) > 1 else parts[0]
            values["sum", g] = sums[g]
        return total([sums[g] for g in granules], 1.0 / scale, amplitudes.shape[0], width)

    special = occ_size == 4 and vir_size == 8
    in_specs = (P("occ", "vir"), P("vir", "occ"), P("occ"), P("vir"))
    return jax.shard_map(
        body if special else plain_body,
        mesh=mesh,
        in_specs=in_specs,
        out_specs=P("occ", "vir"),
        check_vma=False,
    )
```

```python
import functools
import math

import jax
import jax.numpy as jnp
from jax import lax
from jax.experimental import pallas as pl
from jax.experimental.pallas import tpu as pltpu
from jax.sharding import PartitionSpec as P

AMPLITUDE_MAX = 6.0
INTEGRAL_MAX = 0.1875
HALF_MAX = 65504.0
SHARES = (2, 2, 2, 2)
ORDER = (('near', 0), ('rest', 0), ('near', 1), ('far', 0), ('rest', 1), ('near', 2), ('far', 1), ('rest', 2), ('near', 3), ('far', 2), ('rest', 3), ('far', 3))
DEPTH = 4
STRICT = 1
ZSPLIT = (1, 1, 2, 2)
GATES = {('far', 1): [('product', 0)], ('far', 2): [('product', 1)], ('rest', 3): [('pair', 0)], ('product', 2): [('pair', 1)], ('product', 3): [('product', 2)], ('near', 2): ['masked']}
ROW_TILE = 1024
VMEM_LIMIT = 11 * 1024 * 1024


def masked_amplitudes(amplitudes, ij_irrep, cd_irrep):
    rows, columns = ij_irrep.astype(amplitudes.dtype), cd_irrep.astype(amplitudes.dtype)
    return jnp.where(rows[:, None] == columns[None, :], amplitudes, jnp.zeros_like(amplitudes))


def plain_body(amplitudes, integrals, ij_irrep, cd_irrep):
    partial_sums = jnp.dot(
        masked_amplitudes(amplitudes, ij_irrep, cd_irrep),
        lax.all_gather(integrals, "occ", axis=1, tiled=True),
        preferred_element_type=jnp.float32,
    )
    return lax.psum_scatter(partial_sums, "vir", scatter_dimension=1, tiled=True)


def product_kernel(scale, slot_ref, own_amps, other_amps, *refs):
    pieces, out_ref, own_rows, other_rows = refs[:8], refs[8], refs[9], refs[10]
    depth, width = own_rows.shape[0], own_rows.shape[1] // 4
    folds = depth // pieces[0].shape[0]
    part = depth // folds
    for target, blocks in ((own_rows, pieces[0::2]), (other_rows, pieces[1::2])):
        for f in range(folds):
            cut = slice(f * width, (f + 1) * width)
            target[pl.ds(f * part, part), :] = jnp.concatenate([b[:, cut] for b in blocks], axis=1)

    for i in range(own_amps.shape[0] // ROW_TILE):
        at = pl.ds(i * ROW_TILE, ROW_TILE)
        sums = jnp.dot(own_amps[at, :], own_rows[...], preferred_element_type=jnp.float32)
        sums += jnp.dot(other_amps[at, :], other_rows[...], preferred_element_type=jnp.float32)
        sums = sums * scale
        rows = ROW_TILE // folds
        for relation in range(4):
            block = sums[:, relation * width : (relation + 1) * width]
            if folds > 1:
                block = jnp.concatenate([block[f * rows : (f + 1) * rows] for f in range(folds)], axis=1)
            out_ref[slot_ref[relation], pl.ds(i * rows, rows), :] = block


def product(slots, own_amps, other_amps, pieces, scale, depth):
    lanes = pieces[0].shape[1]
    folds = depth // pieces[0].shape[0]
    return pl.pallas_call(
        functools.partial(product_kernel, scale),
        in_specs=[pl.BlockSpec(memory_space=pltpu.SMEM)]
        + [pl.BlockSpec(memory_space=pltpu.VMEM)] * (2 + len(pieces)),
        out_specs=pl.BlockSpec(memory_space=pltpu.VMEM),
        out_shape=jax.ShapeDtypeStruct((4, own_amps.shape[0] // folds, lanes), jnp.float32),
        scratch_shapes=[pltpu.VMEM((depth, 4 * lanes // folds), jnp.bfloat16)] * 2,
        compiler_params=pltpu.CompilerParams(vmem_limit_bytes=VMEM_LIMIT),
        cost_estimate=pl.CostEstimate(flops=0, bytes_accessed=0, transcendentals=0),
    )(slots, own_amps, other_amps, *pieces)


def total_kernel(unscale, *refs):
    parts, out_ref = refs[:-1], refs[-1]
    rows = out_ref.shape[0]
    for i in range(rows // ROW_TILE):
        columns = []
        for part in parts:
            folds = rows // part.shape[0]
            tile = ROW_TILE // folds
            total = part[pl.ds(i * tile, tile), :] * unscale
            width = total.shape[1] // folds
            if folds > 1:
                total = jnp.concatenate([total[:, f * width : (f + 1) * width] for f in range(folds)], axis=0)
            columns.append(total)
        out_ref[pl.ds(i * ROW_TILE, ROW_TILE), :] = jnp.concatenate(columns, axis=1)


def total(parts, unscale, rows, columns):
    return pl.pallas_call(
        functools.partial(total_kernel, unscale),
        in_specs=[pl.BlockSpec(memory_space=pltpu.VMEM)] * len(parts),
        out_specs=pl.BlockSpec(memory_space=pltpu.VMEM),
        out_shape=jax.ShapeDtypeStruct((rows, columns), jnp.float32),
        compiler_params=pltpu.CompilerParams(vmem_limit_bytes=VMEM_LIMIT),
        cost_estimate=pl.CostEstimate(flops=0, bytes_accessed=0, transcendentals=0),
    )(*parts)


def solution(mesh):
    occ_size, vir_size = mesh.shape["occ"], mesh.shape["vir"]
    chips_z = vir_size // 2

    def send(array, target):
        pairs = [
            (o * vir_size + v, target(o, v)[0] * vir_size + target(o, v)[1])
            for o in range(occ_size)
            for v in range(vir_size)
        ]
        return lax.ppermute(array, ("occ", "vir"), pairs)

    to_x = functools.partial(send, target=lambda o, v: (o ^ 1, v))
    to_y = functools.partial(send, target=lambda o, v: (o ^ 2, v))
    to_x_across = functools.partial(send, target=lambda o, v: (o ^ 1, v ^ 1))
    to_y_across = functools.partial(send, target=lambda o, v: (o ^ 2, v ^ 1))
    to_core = functools.partial(send, target=lambda o, v: (o, v ^ 1))

    def along_z(array, hop):
        return send(array, lambda o, v: (o, v ^ (2 * hop)))

    def body(amplitudes, integrals, ij_irrep, cd_irrep):
        depth, columns = integrals.shape
        width = columns // 2
        bound = 4 * depth * AMPLITUDE_MAX * INTEGRAL_MAX
        scale = 2.0 ** math.floor(math.log2(HALF_MAX / bound))
        core = lax.axis_index("vir") % 2
        chip = lax.axis_index("vir") // 2
        owners = lax.axis_index("occ") ^ jnp.arange(4, dtype=jnp.int32)
        hops = owners ^ chip
        ends = [width * sum(SHARES[: g + 1]) // sum(SHARES) for g in range(len(SHARES))]
        granules = range(len(SHARES))

        def piece(array, g):
            cut = array[:, (ends[g - 1] if g else 0) : ends[g]]
            if cut.shape[1] % 128 == 0:
                return cut
            folds = 128 // cut.shape[1]
            return jnp.concatenate(jnp.split(cut, folds), axis=1)

        def columns_of(array, which):
            return lax.dynamic_slice_in_dim(array, which * width, width, axis=1)

        first = (piece(columns_of(integrals, core), 0), piece(columns_of(integrals, 1 - core), 0))
        first, integrals = lax.optimization_barrier((first, integrals))
        mine, theirs = columns_of(integrals, core), columns_of(integrals, 1 - core)
        other_raw = to_core(amplitudes)
        own_amps = masked_amplitudes(amplitudes, ij_irrep, cd_irrep)
        other_amps = masked_amplitudes(other_raw, ij_irrep, to_core(cd_irrep))
        same = [first[0]] + [piece(mine, g) for g in granules[1:]]
        cross = [first[1]] + [piece(theirs, g) for g in granules[1:]]
        swapped = to_core(theirs)
        swapped = [piece(swapped, g) for g in granules]

        values, on_x, on_y, sums = {"masked": (own_amps, other_amps)}, {}, {}, {}
        order = list(ORDER)

        def gated(load, name):
            waits = [values[other] for other in GATES.get(name, ()) if other in values]
            return lax.optimization_barrier((load, waits))[0] if waits else load

        for kind, g in ORDER:
            if kind == "far":
                loads = (on_y["near", g], on_x["near", g])
                ways = (to_x, to_y)
            elif kind == "near":
                loads = (same[g], cross[g])
                ways = (to_x, to_y_across)
            else:
                loads = (cross[g], same[g])
                ways = (to_x_across, to_y)
            loads = gated(loads, (kind, g))
            back = order.index((kind, g)) - DEPTH
            if back >= 0:
                earlier = [values[name] for name in order[max(back - STRICT, 0) : back + 1]]
                loads, _ = lax.optimization_barrier((loads, earlier))
            on_y[kind, g] = ways[1](loads[1])
            on_x[kind, g] = ways[0](loads[0])
            values[kind, g] = (on_x[kind, g], on_y[kind, g])
            if not all((k, g) in on_x for k in ("near", "rest", "far")):
                continue
            pieces = [
                same[g], swapped[g],
                on_x["near", g], on_x["rest", g],
                on_y["rest", g], on_y["near", g],
                on_y["far", g], on_x["far", g],
            ]
            pieces = gated(pieces, ("product", g))
            slots = hops // 2 + 2 * (hops % 2)
            partials = product(slots, own_amps, other_amps, pieces, scale, depth)
            values["product", g] = partials
            parts = []
            for kept in jnp.split(partials, ZSPLIT[g], axis=1):
                pair = kept[:2] + along_z(kept[2:].astype(jnp.float16), 1).astype(jnp.float32)
                parts.append(pair[0] + along_z(pair[1].astype(jnp.float16), 2).astype(jnp.float32))
            values["pair", g] = pair
            sums[g] = jnp.concatenate(parts, axis=0) if len(parts) > 1 else parts[0]
            values["sum", g] = sums[g]
        return total([sums[g] for g in granules], 1.0 / scale, amplitudes.shape[0], width)

    special = occ_size == 4 and vir_size == 8
    in_specs = (P("occ", "vir"), P("vir", "occ"), P("occ"), P("vir"))
    return jax.shard_map(
        body if special else plain_body,
        mesh=mesh,
        in_specs=in_specs,
        out_specs=P("occ", "vir"),
        check_vma=False,
    )
```
